512 devices in a mesh: tok: 16 (over y, x), hid: 8 (over z_lo, core), ffn: 4 (over z_hi).
Axes of the slice: x: 4, y: 4, z: 16 (z_hi: 4, z_lo: 4; z = z_hi * 4 + z_lo), core: 2. Of those that a mesh axis runs over, the one named last changes fastest.
Arguments:
- tokens: bfloat16 [4096, 5120], P('tok', 'hid'), may hold values from -6 to 6
- gate_weight: bfloat16 [5120, 4096], P('hid', ('ffn', 'tok')), may hold values from -0.078125 to 0.078125
- up_weight: bfloat16 [5120, 4096], P('hid', ('ffn', 'tok')), may hold values from -0.078125 to 0.078125
- down_weight: bfloat16 [4096, 5120], P('ffn', 'hid'), may hold values from -0.09375 to 0.09375
- gate_mask: int32 [40, 32], replicated, may hold values 0 or 1
- up_mask: int32 [40, 32], replicated, may hold values 0 or 1
- down_mask: int32 [32, 40], replicated, may hold values 0 or 1
- cotangent: bfloat16 [4096, 5120], P(('tok', 'ffn'), 'hid'), may hold values from -6 to 6
Outputs:
- mixed: bfloat16 [4096, 5120], P(('tok', 'ffn'), 'hid')
- tokens_grad: bfloat16 [4096, 5120], P('tok', 'hid')
- gate_grad: bfloat16 [5120, 4096], P('hid', ('ffn', 'tok'))
- up_grad: bfloat16 [5120, 4096], P('hid', ('ffn', 'tok'))
- down_grad: bfloat16 [4096, 5120], P(('ffn', 'tok'), 'hid')
The draws below stay inside these ranges and needn't reach their ends.
All inputs are finite; a program needn't handle non-finite values.
Results may differ from the reference program's by a relative error of at most 0.018.
Values may be sent and summed in bfloat16 or wider, within the bound.
No kernel may reach another device: no remote copies, remote signals or barrier semaphores. Data moves between devices by JAX's collectives and lax.ppermute only.
A program may use at most 64 MiB of HBM per device.

```python
import jax
import jax.numpy as jnp
from jax import lax

D = 5120
FF = 4096
BLOCK = 128
TOK_DEV = 256
TOKENS = 4096
N_TOK = 16
N_FFN = 4


def plant(array, own_key, smallest, largest):
    longest = array.shape.index(max(array.shape))
    spots = []
    for shift in (0, 1):
        where = [jax.random.randint(jax.random.fold_in(own_key, axis), (), 0, length) for axis, length in enumerate(array.shape)]
        where[longest] = (where[longest] + shift) % array.shape[longest]
        spots.append(tuple(where))
    return array.at[spots[0]].set(smallest).at[spots[1]].set(largest)


def level_of(own_key, dims, split, smallest, high):
    level = 1.0
    for dim, blocks in split:
        steps = jax.random.uniform(jax.random.fold_in(jax.random.fold_in(own_key, 6), dim), (blocks,), jnp.float32, smallest / len(split), high / len(split))
        level = level * jnp.repeat(jnp.exp(steps), dims[dim] // blocks).reshape((-1,) + (1,) * (len(dims) - 1 - dim))
    return level


def bell_draw(stream_key, shape, scale, most, cuts=(), kind=jnp.bfloat16):
    result = scale * jax.random.normal(stream_key, shape, jnp.float32)
    if cuts:
        result = result * level_of(stream_key, shape, cuts, -0.22, 0.18)
    return jnp.clip(result, -most, most).astype(kind)


def setup_inputs(seed: int = 0) -> dict:
    streams_of = jax.random.split(jax.random.key(seed), 9)
    return {
        "tokens": bell_draw(streams_of[0], (TOKENS, D), 1.0, 6.0, ((0, 16), (1, 8))),
        "gate_weight": bell_draw(streams_of[1], (D, FF), D ** -0.5, 0.078125, ((0, 8), (1, 64))),
        "up_weight": bell_draw(streams_of[2], (D, FF), D ** -0.5, 0.078125, ((0, 8), (1, 64))),
        "down_weight": bell_draw(streams_of[3], (FF, D), FF ** -0.5, 0.09375, ((0, 4), (1, 8))),
        "gate_mask": plant((jax.random.randint(streams_of[4], (D // BLOCK, FF // BLOCK), 0, 10) < 3).astype(jnp.int32), jax.random.fold_in(streams_of[4], 1), 0, 1),
        "up_mask": plant((jax.random.randint(streams_of[5], (D // BLOCK, FF // BLOCK), 0, 10) < 3).astype(jnp.int32), jax.random.fold_in(streams_of[5], 1), 0, 1),
        "down_mask": plant((jax.random.randint(streams_of[6], (FF // BLOCK, D // BLOCK), 0, 10) < 3).astype(jnp.int32), jax.random.fold_in(streams_of[6], 1), 0, 1),
        "cotangent": bell_draw(streams_of[7], (TOKENS, D), 1.0, 6.0, ((0, 64), (1, 8))),
    }


def expand(blocks):
    return jnp.repeat(jnp.repeat(blocks, BLOCK, axis=0), BLOCK, axis=1).astype(jnp.bfloat16)


def rounded(value):
    return lax.optimization_barrier(value.astype(jnp.bfloat16)).astype(jnp.float32)


def reference(tokens, gate_weight, up_weight, down_weight, gate_mask, up_mask, down_mask, cotangent):
    gate_keep = expand(gate_mask)
    up_keep = expand(up_mask)
    down_keep = expand(down_mask)
    gate_eff = gate_weight * gate_keep
    up_eff = up_weight * up_keep
    down_eff = down_weight * down_keep
    gate = jnp.dot(tokens, gate_eff, preferred_element_type=jnp.float32)
    up = jnp.dot(tokens, up_eff, preferred_element_type=jnp.float32)
    hidden = (jax.nn.silu(gate) * up).astype(jnp.bfloat16)
    width = FF // N_FFN
    mixed = jnp.zeros((TOKENS, D), jnp.float32)
    for group in range(N_FFN):
        term = jnp.dot(hidden[:, group * width:(group + 1) * width], down_eff[group * width:(group + 1) * width], preferred_element_type=jnp.float32)
        mixed = mixed + rounded(term)
    mixed = mixed.astype(jnp.bfloat16)
    hidden_grad = jnp.dot(cotangent, down_eff.T, preferred_element_type=jnp.float32)
    sigma = jax.nn.sigmoid(gate)
    gate_delta = (hidden_grad * up * sigma * (1.0 + gate * (1.0 - sigma))).astype(jnp.bfloat16)
    up_delta = (hidden_grad * gate * sigma).astype(jnp.bfloat16)
    gate_sum = jnp.zeros((D, FF), jnp.float32)
    up_sum = jnp.zeros((D, FF), jnp.float32)
    down_sum = jnp.zeros((FF, D), jnp.float32)
    for group in range(N_TOK):
        rows = slice(group * TOK_DEV, (group + 1) * TOK_DEV)
        gate_sum = gate_sum + rounded(jnp.dot(tokens[rows].T, gate_delta[rows], preferred_element_type=jnp.float32))
        up_sum = up_sum + rounded(jnp.dot(tokens[rows].T, up_delta[rows], preferred_element_type=jnp.float32))
        down_sum = down_sum + rounded(jnp.dot(hidden[rows].T, cotangent[rows], preferred_element_type=jnp.float32))
    scale = 1.0 / N_TOK
    gate_grad = (gate_keep.astype(jnp.float32) * gate_sum * scale).astype(jnp.bfloat16)
    up_grad = (up_keep.astype(jnp.float32) * up_sum * scale).astype(jnp.bfloat16)
    down_grad = (down_keep.astype(jnp.float32) * down_sum * scale).astype(jnp.bfloat16)
    tokens_grad = jnp.dot(gate_delta, gate_eff.T, preferred_element_type=jnp.float32)
    tokens_grad = tokens_grad + jnp.dot(up_delta, up_eff.T, preferred_element_type=jnp.float32)
    return mixed, tokens_grad.astype(jnp.bfloat16), gate_grad, up_grad, down_grad
```

```python
import jax
import jax.numpy as jnp
from jax import lax
from jax.experimental import pallas as pl
from jax.experimental.pallas import tpu as pltpu
from jax.sharding import PartitionSpec as P

BLOCK = 128
BF = jnp.bfloat16
F32 = jnp.float32
CHIPS_Y = 4


def dot(left, right, left_axis, right_axis):
    return lax.dot_general(
        left, right, (((left_axis,), (right_axis,)), ((), ())), preferred_element_type=F32
    )


def total(parts):
    return jnp.sum(parts.astype(F32), axis=0)


def pick(parts, index):
    return lax.dynamic_index_in_dim(parts, index, 0, keepdims=False)


def keep_rows(mask, row_first, row_blocks, col_first, col_blocks):
    part = lax.dynamic_slice(mask, (row_first, col_first), (row_blocks, col_blocks))
    return jnp.repeat(part.astype(BF), BLOCK, axis=1)


def activation_kernel(own, units, part_ref, out_ref):
    for k in range(units // own):
        at = 2 * own * k
        gate = total(part_ref[:, :, at : at + own])
        up = total(part_ref[:, :, at + own : at + 2 * own])
        hidden_grad = total(part_ref[:, :, 2 * units + own * k : 2 * units + own * (k + 1)])
        sigma = jax.nn.sigmoid(gate)
        out_ref[:, 2 * units + own * k : 2 * units + own * (k + 1)] = (gate * sigma * up).astype(BF)
        out_ref[:, at : at + own] = (
            hidden_grad * up * sigma * (1.0 + gate * (1.0 - sigma))
        ).astype(BF)
        out_ref[:, at + own : at + 2 * own] = (hidden_grad * gate * sigma).astype(BF)


def activation(own, units, parts):
    count = parts.shape[1]
    return pl.pallas_call(
        lambda *refs: activation_kernel(own, units, *refs),
        out_shape=jax.ShapeDtypeStruct((count, 3 * units), BF),
        in_specs=[pl.BlockSpec(memory_space=pltpu.VMEM)],
        out_specs=pl.BlockSpec(memory_space=pltpu.VMEM),
        compiler_params=pltpu.CompilerParams(vmem_limit_bytes=16 * 2**20),
        cost_estimate=pl.CostEstimate(
            flops=20 * count * units, bytes_accessed=30 * count * units, transcendentals=count * units
        ),
    )(parts)


def body(tokens, gate_weight, up_weight, down_weight, gate_mask, up_mask, down_mask, cotangent):
    n_tok, n_hid, n_ffn = (lax.axis_size(a) for a in ("tok", "hid", "ffn"))
    t, h, f = (lax.axis_index(a) for a in ("tok", "hid", "ffn"))
    rows, feats = tokens.shape
    units = down_weight.shape[0]
    own = units // n_tok
    feat_blocks, unit_blocks = feats // BLOCK, units // BLOCK
    n_line = n_hid // 2
    c = h % 2
    n_y = CHIPS_Y
    n_x = n_tok // n_y
    pairs = [[2 * i + j for j in range(2)] for i in range(n_line)]
    lines = [[2 * i + j for i in range(n_line)] for j in range(2)]
    along_y = [[n_x * i + j for i in range(n_y)] for j in range(n_x)]
    along_x = [[n_x * i + j for j in range(n_x)] for i in range(n_y)]

    def hop_hid(value, distance):
        return lax.ppermute(value, "hid", [(i, i ^ distance) for i in range(n_hid)])

    own_block = (f * units + t * own) // BLOCK
    keep_gate = keep_rows(gate_mask.T, own_block, 1, h * feat_blocks, feat_blocks)
    keep_up = keep_rows(up_mask.T, own_block, 1, h * feat_blocks, feat_blocks)
    keep_own_down = keep_rows(down_mask, own_block, 1, h * feat_blocks, feat_blocks)
    keep_down = keep_rows(down_mask, f * unit_blocks, unit_blocks, h * feat_blocks, feat_blocks)
    down_eff = (down_weight.reshape(unit_blocks, BLOCK, feats) * keep_down[:, None, :]).reshape(
        units, feats
    )

    is_gate = lax.broadcasted_iota(jnp.int32, (n_tok, 2, own, feats), 1) == 0
    spread = jnp.where(is_gate, (gate_weight.T * keep_gate)[None, None], (up_weight.T * keep_up)[None, None])
    spread = spread.reshape(n_tok, 2 * own, feats)
    weights = lax.all_to_all(spread, "tok", 0, 0).reshape(2 * units, feats)
    grad_rows = lax.all_gather(cotangent, "ffn", axis=0, tiled=True)

    def gather_y(array):
        return lax.all_gather(array, "tok", axis=0, tiled=True, axis_index_groups=along_y)

    tokens_y = gather_y(tokens)

    def sum_cores(part):
        part = part.astype(BF).reshape(2, rows // 2, part.shape[1])
        half = pick(part, c).astype(F32) + hop_hid(pick(part, 1 - c), 1).astype(F32)
        return half.astype(BF).reshape(n_line, rows // n_hid, part.shape[2])

    grad_half = sum_cores(dot(grad_rows, down_eff, 1, 1))
    weights, grad_half = lax.optimization_barrier((weights, grad_half))
    both_half = sum_cores(dot(tokens, weights, 1, 1))
    parts = lax.all_to_all(
        jnp.concatenate([both_half, grad_half], axis=2), "hid", 0, 0, axis_index_groups=lines
    )
    acts = activation(own, units, parts)
    mine = lax.all_gather(acts, "hid", axis=0, tiled=True, axis_index_groups=lines)
    mine, tokens_y = lax.optimization_barrier((mine, tokens_y))
    other = hop_hid(mine, 1)

    def in_order(first, last):
        halves = mine[:, first:last], other[:, first:last]
        return jnp.concatenate([jnp.where(c == k, *halves) for k in range(2)])

    deltas = in_order(0, 2 * units)
    hidden = in_order(2 * units, 3 * units)

    def exchange(parts, groups=None):
        return lax.all_to_all(parts, "tok", 0, 0, axis_index_groups=groups)

    quarter = deltas.reshape(rows, n_y, 2 * units // n_y).transpose(1, 0, 2)
    quarter = exchange(quarter, along_y).reshape(n_y * rows, 2 * units // n_y)

    def beside(i):
        return i ^ 1

    def around(i):
        return n_ffn - 1 - i

    def swap(values, pairing):
        sent = jnp.concatenate(values)
        return lax.ppermute(sent, "ffn", [(i, pairing(i)) for i in range(n_ffn)])

    def plus(left, right):
        return (left.astype(F32) + right.astype(F32)).astype(BF)

    input_part = dot(deltas, weights, 1, 0).astype(BF).reshape(2, rows // 2, feats)
    mixed_part = dot(hidden, down_eff, 1, 0).astype(BF)
    mixed_part = mixed_part.reshape(n_ffn, 2, rows // n_ffn // 2, feats)
    half, block = rows // 2, rows // n_ffn // 2
    pairings = ((beside, around), (around, beside))
    waiting = []
    for k, (first, second) in enumerate(pairings):
        piece = mixed_part[:, k]
        got = swap([input_part[k], pick(piece, first(f)), pick(piece, second(first(f)))], first)
        waiting.append(
            (
                plus(input_part[k], got[:half]),
                plus(pick(piece, f), got[half : half + block]),
                plus(pick(piece, second(f)), got[half + block :]),
            )
        )
    waiting, quarter = lax.optimization_barrier((waiting, quarter))
    input_sums, mixed_sums = [], []
    for (first, second), (input_sum, own_sum, sent_sum) in zip(pairings, waiting):
        got = swap([input_sum, sent_sum], second)
        input_sums.append(plus(input_sum, got[:half]))
        mixed_sums.append(plus(own_sum, got[half:]))
    tokens_grad = jnp.concatenate(input_sums)
    mixed = jnp.concatenate(mixed_sums)

    down_term = dot(hidden, grad_rows, 0, 0).astype(BF).reshape(n_tok, own, feats)
    down_sum = total(exchange(down_term)) * (1.0 / n_tok)
    delta_term = dot(quarter, tokens_y, 0, 0).astype(BF).reshape(n_x, 2 * own, feats)
    sums = total(exchange(delta_term, along_x)) * (1.0 / n_tok)
    gate_grad = (sums[:own] * keep_gate.astype(F32)).astype(BF).T
    up_grad = (sums[own:] * keep_up.astype(F32)).astype(BF).T
    down_grad = (down_sum * keep_own_down.astype(F32)).astype(BF)
    return (mixed, tokens_grad, gate_grad, up_grad, down_grad)


def solution(mesh):
    in_specs = (
        P("tok", "hid"),
        P("hid", ("ffn", "tok")),
        P("hid", ("ffn", "tok")),
        P("ffn", "hid"),
        P(),
        P(),
        P(),
        P(("tok", "ffn"), "hid"),
    )
    out_specs = (
        P(("tok", "ffn"), "hid"),
        P("tok", "hid"),
        P("hid", ("ffn", "tok")),
        P("hid", ("ffn", "tok")),
        P(("ffn", "tok"), "hid"),
    )
    return jax.shard_map(body, mesh=mesh, in_specs=in_specs, out_specs=out_specs, check_vma=False)
```

```python
import jax
import jax.numpy as jnp
from jax import lax
from jax.experimental import pallas as pl
from jax.experimental.pallas import tpu as pltpu
from jax.sharding import PartitionSpec as P

BLOCK = 128
BF = jnp.bfloat16
F32 = jnp.float32


def dot(left, right, left_axis, right_axis):
    return lax.dot_general(
        left, right, (((left_axis,), (right_axis,)), ((), ())), preferred_element_type=F32
    )


def total(parts):
    return jnp.sum(parts.astype(F32), axis=0)


def pick(parts, index):
    return lax.dynamic_index_in_dim(parts, index, 0, keepdims=False)


def keep_rows(mask, row_first, row_blocks, col_first, col_blocks):
    part = lax.dynamic_slice(mask, (row_first, col_first), (row_blocks, col_blocks))
    return jnp.repeat(part.astype(BF), BLOCK, axis=1)


def activation_kernel(own, units, part_ref, out_ref):
    for k in range(units // own):
        at = 2 * own * k
        gate = total(part_ref[:, :, at : at + own])
        up = total(part_ref[:, :, at + own : at + 2 * own])
        hidden_grad = total(part_ref[:, :, 2 * units + own * k : 2 * units + own * (k + 1)])
        sigma = jax.nn.sigmoid(gate)
        out_ref[:, 2 * units + own * k : 2 * units + own * (k + 1)] = (gate * sigma * up).astype(BF)
        out_ref[:, at : at + own] = (
            hidden_grad * up * sigma * (1.0 + gate * (1.0 - sigma))
        ).astype(BF)
        out_ref[:, at + own : at + 2 * own] = (hidden_grad * gate * sigma).astype(BF)


def activation(own, units, parts):
    count = parts.shape[1]
    return pl.pallas_call(
        lambda *refs: activation_kernel(own, units, *refs),
        out_shape=jax.ShapeDtypeStruct((count, 3 * units), BF),
        in_specs=[pl.BlockSpec(memory_space=pltpu.VMEM)],
        out_specs=pl.BlockSpec(memory_space=pltpu.VMEM),
        compiler_params=pltpu.CompilerParams(vmem_limit_bytes=16 * 2**20),
        cost_estimate=pl.CostEstimate(
            flops=20 * count * units, bytes_accessed=30 * count * units, transcendentals=count * units
        ),
    )(parts)


def body(tokens, gate_weight, up_weight, down_weight, gate_mask, up_mask, down_mask, cotangent):
    n_tok, n_hid, n_ffn = (lax.axis_size(a) for a in ("tok", "hid", "ffn"))
    t, h, f = (lax.axis_index(a) for a in ("tok", "hid", "ffn"))
    rows, feats = tokens.shape
    units = down_weight.shape[0]
    own = units // n_tok
    feat_blocks, unit_blocks = feats // BLOCK, units // BLOCK
    n_line = n_hid // 2
    c = h % 2
    pairs = [[2 * i + j for j in range(2)] for i in range(n_line)]
    lines = [[2 * i + j for i in range(n_line)] for j in range(2)]

    def hop_hid(value, distance):
        return lax.ppermute(value, "hid", [(i, i ^ distance) for i in range(n_hid)])

    own_block = (f * units + t * own) // BLOCK
    keep_gate = keep_rows(gate_mask.T, own_block, 1, h * feat_blocks, feat_blocks)
    keep_up = keep_rows(up_mask.T, own_block, 1, h * feat_blocks, feat_blocks)
    keep_own_down = keep_rows(down_mask, own_block, 1, h * feat_blocks, feat_blocks)
    keep_down = keep_rows(down_mask, f * unit_blocks, unit_blocks, h * feat_blocks, feat_blocks)
    down_eff = (down_weight.reshape(unit_blocks, BLOCK, feats) * keep_down[:, None, :]).reshape(
        units, feats
    )

    is_gate = lax.broadcasted_iota(jnp.int32, (n_tok, 2, own, feats), 1) == 0
    spread = jnp.where(is_gate, (gate_weight.T * keep_gate)[None, None], (up_weight.T * keep_up)[None, None])
    spread = spread.reshape(n_tok, 2 * own, feats)
    weights = lax.all_to_all(spread, "tok", 0, 0).reshape(2 * units, feats)
    grad_rows = lax.all_gather(cotangent, "ffn", axis=0, tiled=True)

    def sum_cores(part):
        part = part.astype(BF).reshape(2, rows // 2, part.shape[1])
        half = pick(part, c).astype(F32) + hop_hid(pick(part, 1 - c), 1).astype(F32)
        return half.astype(BF).reshape(n_line, rows // n_hid, part.shape[2])

    grad_half = sum_cores(dot(grad_rows, down_eff, 1, 1))
    weights, grad_half = lax.optimization_barrier((weights, grad_half))
    both_half = sum_cores(dot(tokens, weights, 1, 1))
    parts = lax.all_to_all(
        jnp.concatenate([both_half, grad_half], axis=2), "hid", 0, 0, axis_index_groups=lines
    )
    acts = activation(own, units, parts)
    mine = lax.all_gather(acts, "hid", axis=0, tiled=True, axis_index_groups=lines)
    other = hop_hid(mine, 1)

    def in_order(first, last):
        halves = mine[:, first:last], other[:, first:last]
        return jnp.concatenate([jnp.where(c == k, *halves) for k in range(2)])

    deltas = in_order(0, 2 * units)
    hidden = in_order(2 * units, 3 * units)

    delta_term = dot(deltas, tokens, 0, 0).astype(BF).reshape(n_tok, 2 * own, feats)
    down_term = dot(hidden, grad_rows, 0, 0).astype(BF).reshape(n_tok, own, feats)
    terms = lax.all_to_all(jnp.concatenate([delta_term, down_term], axis=1), "tok", 0, 0)
    sums = total(terms) * (1.0 / n_tok)

    def beside(i):
        return i ^ 1

    def around(i):
        return n_ffn - 1 - i

    def swap(values, pairing):
        sent = jnp.concatenate(values)
        return lax.ppermute(sent, "ffn", [(i, pairing(i)) for i in range(n_ffn)])

    def plus(left, right):
        return (left.astype(F32) + right.astype(F32)).astype(BF)

    input_part = dot(deltas, weights, 1, 0).astype(BF).reshape(2, rows // 2, feats)
    mixed_part = dot(hidden, down_eff, 1, 0).astype(BF)
    mixed_part = mixed_part.reshape(n_ffn, 2, rows // n_ffn // 2, feats)
    half, block = rows // 2, rows // n_ffn // 2
    pairings = ((beside, around), (around, beside))
    waiting = []
    for k, (first, second) in enumerate(pairings):
        piece = mixed_part[:, k]
        got = swap([input_part[k], pick(piece, first(f)), pick(piece, second(first(f)))], first)
        waiting.append(
            (
                plus(input_part[k], got[:half]),
                plus(pick(piece, f), got[half : half + block]),
                plus(pick(piece, second(f)), got[half + block :]),
            )
        )
    input_sums, mixed_sums = [], []
    for (first, second), (input_sum, own_sum, sent_sum) in zip(pairings, waiting):
        got = swap([input_sum, sent_sum], second)
        input_sums.append(plus(input_sum, got[:half]))
        mixed_sums.append(plus(own_sum, got[half:]))
    tokens_grad = jnp.concatenate(input_sums)
    mixed = jnp.concatenate(mixed_sums)

    gate_grad = (sums[:own] * keep_gate.astype(F32)).astype(BF).T
    up_grad = (sums[own : 2 * own] * keep_up.astype(F32)).astype(BF).T
    down_grad = (sums[2 * own :] * keep_own_down.astype(F32)).astype(BF)
    return (mixed, tokens_grad, gate_grad, up_grad, down_grad)


def solution(mesh):
    in_specs = (
        P("tok", "hid"),
        P("hid", ("ffn", "tok")),
        P("hid", ("ffn", "tok")),
        P("ffn", "hid"),
        P(),
        P(),
        P(),
        P(("tok", "ffn"), "hid"),
    )
    out_specs = (
        P(("tok", "ffn"), "hid"),
        P("tok", "hid"),
        P("hid", ("ffn", "tok")),
        P("hid", ("ffn", "tok")),
        P(("ffn", "tok"), "hid"),
    )
    return jax.shard_map(body, mesh=mesh, in_specs=in_specs, out_specs=out_specs, check_vma=False)
```

```python
import jax
import jax.numpy as jnp
from jax import lax
from jax.experimental import pallas as pl
from jax.experimental.pallas import tpu as pltpu
from jax.sharding import PartitionSpec as P

BLOCK = 128
BF = jnp.bfloat16
F32 = jnp.float32


def dot(left, right, left_axis, right_axis):
    return lax.dot_general(
        left, right, (((left_axis,), (right_axis,)), ((), ())), preferred_element_type=F32
    )


def total(parts):
    return jnp.sum(parts.astype(F32), axis=0)


def pick(parts, index):
    return lax.dynamic_index_in_dim(parts, index, 0, keepdims=False)


def keep_rows(mask, row_first, row_blocks, col_first, col_blocks):
    part = lax.dynamic_slice(mask, (row_first, col_first), (row_blocks, col_blocks))
    return jnp.repeat(part.astype(BF), BLOCK, axis=1)


def activation_kernel(own, units, part_ref, out_ref):
    for k in range(units // own):
        at = 2 * own * k
        gate = total(part_ref[:, :, at : at + own])
        up = total(part_ref[:, :, at + own : at + 2 * own])
        hidden_grad = total(part_ref[:, :, 2 * units + own * k : 2 * units + own * (k + 1)])
        sigma = jax.nn.sigmoid(gate)
        out_ref[:, 2 * units + own * k : 2 * units + own * (k + 1)] = (gate * sigma * up).astype(BF)
        out_ref[:, at : at + own] = (
            hidden_grad * up * sigma * (1.0 + gate * (1.0 - sigma))
        ).astype(BF)
        out_ref[:, at + own : at + 2 * own] = (hidden_grad * gate * sigma).astype(BF)


def activation(own, units, parts):
    count = parts.shape[1]
    return pl.pallas_call(
        lambda *refs: activation_kernel(own, units, *refs),
        out_shape=jax.ShapeDtypeStruct((count, 3 * units), BF),
        in_specs=[pl.BlockSpec(memory_space=pltpu.VMEM)],
        out_specs=pl.BlockSpec(memory_space=pltpu.VMEM),
        compiler_params=pltpu.CompilerParams(vmem_limit_bytes=16 * 2**20),
        cost_estimate=pl.CostEstimate(
            flops=20 * count * units, bytes_accessed=30 * count * units, transcendentals=count * units
        ),
    )(parts)


def body(tokens, gate_weight, up_weight, down_weight, gate_mask, up_mask, down_mask, cotangent):
    n_tok, n_hid, n_ffn = (lax.axis_size(a) for a in ("tok", "hid", "ffn"))
    t, h, f = (lax.axis_index(a) for a in ("tok", "hid", "ffn"))
    rows, feats = tokens.shape
    units = down_weight.shape[0]
    own = units // n_tok
    feat_blocks, unit_blocks = feats // BLOCK, units // BLOCK
    n_line = n_hid // 2
    c = h % 2
    pairs = [[2 * i + j for j in range(2)] for i in range(n_line)]
    lines = [[2 * i + j for i in range(n_line)] for j in range(2)]

    def hop_hid(value, distance):
        return lax.ppermute(value, "hid", [(i, i ^ distance) for i in range(n_hid)])

    own_block = (f * units + t * own) // BLOCK
    keep_gate = keep_rows(gate_mask.T, own_block, 1, h * feat_blocks, feat_blocks)
    keep_up = keep_rows(up_mask.T, own_block, 1, h * feat_blocks, feat_blocks)
    keep_own_down = keep_rows(down_mask, own_block, 1, h * feat_blocks, feat_blocks)
    keep_down = keep_rows(down_mask, f * unit_blocks, unit_blocks, h * feat_blocks, feat_blocks)
    down_eff = (down_weight.reshape(unit_blocks, BLOCK, feats) * keep_down[:, None, :]).reshape(
        units, feats
    )

    spread = jnp.broadcast_to(
        jnp.concatenate([gate_weight.T, up_weight.T])[None], (n_tok, 2 * own, feats)
    )
    gathered = lax.all_to_all(spread, "tok", 0, 0)
    first_block = f * unit_blocks
    keep_both = jnp.stack(
        [
            keep_rows(mask.T, first_block, unit_blocks, h * feat_blocks, feat_blocks)
            for mask in (gate_mask, up_mask)
        ],
        axis=1,
    )
    keep_both = jnp.repeat(keep_both, n_tok // unit_blocks, axis=0)
    grad_rows = lax.all_gather(cotangent, "ffn", axis=0, tiled=True)

    def sum_cores(part):
        part = part.astype(BF).reshape(2, rows // 2, part.shape[1])
        half = pick(part, c).astype(F32) + hop_hid(pick(part, 1 - c), 1).astype(F32)
        return half.astype(BF).reshape(n_line, rows // n_hid, part.shape[2])

    grad_half = sum_cores(dot(grad_rows, down_eff, 1, 1))
    gathered, grad_half = lax.optimization_barrier((gathered, grad_half))
    weights = gathered.reshape(n_tok, 2, own, feats) * keep_both[:, :, None, :]
    weights = weights.reshape(2 * units, feats)
    both_half = sum_cores(dot(tokens, weights, 1, 1))
    parts = lax.all_to_all(
        jnp.concatenate([both_half, grad_half], axis=2), "hid", 0, 0, axis_index_groups=lines
    )
    acts = activation(own, units, parts)
    mine = lax.all_gather(acts, "hid", axis=0, tiled=True, axis_index_groups=lines)
    other = hop_hid(mine, 1)

    def in_order(first, last):
        halves = mine[:, first:last], other[:, first:last]
        return jnp.concatenate([jnp.where(c == k, *halves) for k in range(2)])

    deltas = in_order(0, 2 * units)
    hidden = in_order(2 * units, 3 * units)

    delta_term = dot(deltas, tokens, 0, 0).astype(BF).reshape(n_tok, 2 * own, feats)
    down_term = dot(hidden, grad_rows, 0, 0).astype(BF).reshape(n_tok, own, feats)
    terms = lax.all_to_all(jnp.concatenate([delta_term, down_term], axis=1), "tok", 0, 0)
    sums = total(terms) * (1.0 / n_tok)

    def beside(i):
        return i ^ 1

    def around(i):
        return n_ffn - 1 - i

    def swap(values, by_core):
        perm = [
            (j * n_ffn + i, j * n_ffn + by_core[j % 2](i)) for j in range(n_hid) for i in range(n_ffn)
        ]
        return lax.ppermute(jnp.concatenate(values), ("hid", "ffn"), perm)

    def plus(left, right):
        return (left.astype(F32) + right.astype(F32)).astype(BF)

    first = jnp.where(c == 0, beside(f), around(f))
    second = jnp.where(c == 0, around(f), beside(f))
    across = n_ffn - 1 - beside(f)
    block = rows // n_ffn
    input_part = dot(deltas, weights, 1, 0).astype(BF)
    mixed_part = dot(hidden, down_eff, 1, 0).astype(BF).reshape(n_ffn, block, feats)
    got = swap([input_part, pick(mixed_part, first), pick(mixed_part, across)], (beside, around))
    input_sum = plus(input_part, got[:rows])
    own_sum = plus(pick(mixed_part, f), got[rows : rows + block])
    sent_sum = plus(pick(mixed_part, second), got[rows + block :])
    got = swap([input_sum, sent_sum], (around, beside))
    got, sums = lax.optimization_barrier((got, sums))
    tokens_grad = plus(input_sum, got[:rows])
    mixed = plus(own_sum, got[rows:])

    gate_grad = (sums[:own] * keep_gate.astype(F32)).astype(BF).T
    up_grad = (sums[own : 2 * own] * keep_up.astype(F32)).astype(BF).T
    down_grad = (sums[2 * own :] * keep_own_down.astype(F32)).astype(BF)
    return (mixed, tokens_grad, gate_grad, up_grad, down_grad)


def solution(mesh):
    in_specs = (
        P("tok", "hid"),
        P("hid", ("ffn", "tok")),
        P("hid", ("ffn", "tok")),
        P("ffn", "hid"),
        P(),
        P(),
        P(),
        P(("tok", "ffn"), "hid"),
    )
    out_specs = (
        P(("tok", "ffn"), "hid"),
        P("tok", "hid"),
        P("hid", ("ffn", "tok")),
        P("hid", ("ffn", "tok")),
        P(("ffn", "tok"), "hid"),
    )
    return jax.shard_map(body, mesh=mesh, in_specs=in_specs, out_specs=out_specs, check_vma=False)
```

```python
import jax
import jax.numpy as jnp
from jax import lax
from jax.experimental import pallas as pl
from jax.experimental.pallas import tpu as pltpu
from jax.sharding import PartitionSpec as P

BLOCK = 128
BF = jnp.bfloat16
F32 = jnp.float32


def dot(left, right, left_axis, right_axis):
    return lax.dot_general(
        left, right, (((left_axis,), (right_axis,)), ((), ())), preferred_element_type=F32
    )


def total(parts):
    return jnp.sum(parts.astype(F32), axis=0)


def pick(parts, index):
    return lax.dynamic_index_in_dim(parts, index, 0, keepdims=False)


def keep_rows(mask, row_first, row_blocks, col_first, col_blocks):
    part = lax.dynamic_slice(mask, (row_first, col_first), (row_blocks, col_blocks))
    return jnp.repeat(part.astype(BF), BLOCK, axis=1)


def activation_kernel(own, units, part_ref, out_ref):
    for k in range(units // own):
        at = 2 * own * k
        gate = total(part_ref[:, :, at : at + own])
        up = total(part_ref[:, :, at + own : at + 2 * own])
        hidden_grad = total(part_ref[:, :, 2 * units + own * k : 2 * units + own * (k + 1)])
        sigma = jax.nn.sigmoid(gate)
        out_ref[:, 2 * units + own * k : 2 * units + own * (k + 1)] = (gate * sigma * up).astype(BF)
        out_ref[:, at : at + own] = (
            hidden_grad * up * sigma * (1.0 + gate * (1.0 - sigma))
        ).astype(BF)
        out_ref[:, at + own : at + 2 * own] = (hidden_grad * gate * sigma).astype(BF)


def activation(own, units, parts):
    count = parts.shape[1]
    return pl.pallas_call(
        lambda *refs: activation_kernel(own, units, *refs),
        out_shape=jax.ShapeDtypeStruct((count, 3 * units), BF),
        in_specs=[pl.BlockSpec(memory_space=pltpu.VMEM)],
        out_specs=pl.BlockSpec(memory_space=pltpu.VMEM),
        compiler_params=pltpu.CompilerParams(vmem_limit_bytes=16 * 2**20),
        cost_estimate=pl.CostEstimate(
            flops=20 * count * units, bytes_accessed=30 * count * units, transcendentals=count * units
        ),
    )(parts)


def body(tokens, gate_weight, up_weight, down_weight, gate_mask, up_mask, down_mask, cotangent):
    n_tok, n_hid, n_ffn = (lax.axis_size(a) for a in ("tok", "hid", "ffn"))
    t, h, f = (lax.axis_index(a) for a in ("tok", "hid", "ffn"))
    rows, feats = tokens.shape
    units = down_weight.shape[0]
    own = units // n_tok
    feat_blocks, unit_blocks = feats // BLOCK, units // BLOCK
    n_line = n_hid // 2
    c = h % 2
    pairs = [[2 * i + j for j in range(2)] for i in range(n_line)]
    lines = [[2 * i + j for i in range(n_line)] for j in range(2)]

    def hop_hid(value, distance):
        return lax.ppermute(value, "hid", [(i, i ^ distance) for i in range(n_hid)])

    own_block = (f * units + t * own) // BLOCK
    keep_gate = keep_rows(gate_mask.T, own_block, 1, h * feat_blocks, feat_blocks)
    keep_up = keep_rows(up_mask.T, own_block, 1, h * feat_blocks, feat_blocks)
    keep_own_down = keep_rows(down_mask, own_block, 1, h * feat_blocks, feat_blocks)
    keep_down = keep_rows(down_mask, f * unit_blocks, unit_blocks, h * feat_blocks, feat_blocks)
    down_eff = (down_weight.reshape(unit_blocks, BLOCK, feats) * keep_down[:, None, :]).reshape(
        units, feats
    )

    spread = jnp.broadcast_to(
        jnp.concatenate([gate_weight.T, up_weight.T])[None], (n_tok, 2 * own, feats)
    )
    gathered = lax.all_to_all(spread, "tok", 0, 0)
    first_block = f * unit_blocks
    keep_both = jnp.stack(
        [
            keep_rows(mask.T, first_block, unit_blocks, h * feat_blocks, feat_blocks)
            for mask in (gate_mask, up_mask)
        ],
        axis=1,
    )
    keep_both = jnp.repeat(keep_both, n_tok // unit_blocks, axis=0)
    grad_rows = lax.all_gather(cotangent, "ffn", axis=0, tiled=True)

    def sum_cores(part):
        part = part.astype(BF).reshape(2, rows // 2, part.shape[1])
        half = pick(part, c).astype(F32) + hop_hid(pick(part, 1 - c), 1).astype(F32)
        return half.astype(BF).reshape(n_line, rows // n_hid, part.shape[2])

    grad_half = sum_cores(dot(grad_rows, down_eff, 1, 1))
    gathered, grad_half = lax.optimization_barrier((gathered, grad_half))
    weights = gathered.reshape(n_tok, 2, own, feats) * keep_both[:, :, None, :]
    weights = weights.reshape(2 * units, feats)
    both_half = sum_cores(dot(tokens, weights, 1, 1))
    def trade(value, by_core):
        return lax.ppermute(value, "hid", [(i, i ^ (2 * by_core[i % 2])) for i in range(n_hid)])

    z = h // 2
    halves = jnp.concatenate([both_half, grad_half], axis=2)
    near, far = z ^ jnp.where(c == 0, 2, 1), z ^ jnp.where(c == 0, 1, 2)
    got = trade(jnp.stack([pick(halves, near), pick(halves, z ^ 3)]), (2, 1))
    sent_sum = (pick(halves, far).astype(F32) + got[1].astype(F32)).astype(BF)
    parts = jnp.stack([pick(halves, z), got[0], trade(sent_sum, (1, 2))])
    acts = activation(own, units, parts)
    mine = lax.all_gather(acts, "hid", axis=0, tiled=True, axis_index_groups=lines)
    other = hop_hid(mine, 1)

    def in_order(first, last):
        halves = mine[:, first:last], other[:, first:last]
        return jnp.concatenate([jnp.where(c == k, *halves) for k in range(2)])

    deltas = in_order(0, 2 * units)
    hidden = in_order(2 * units, 3 * units)

    delta_term = dot(deltas, tokens, 0, 0).astype(BF).reshape(n_tok, 2 * own, feats)
    down_term = dot(hidden, grad_rows, 0, 0).astype(BF).reshape(n_tok, own, feats)
    terms = lax.all_to_all(jnp.concatenate([delta_term, down_term], axis=1), "tok", 0, 0)
    sums = total(terms) * (1.0 / n_tok)

    def beside(i):
        return i ^ 1

    def around(i):
        return n_ffn - 1 - i

    def swap(values, by_core):
        perm = [
            (j * n_ffn + i, j * n_ffn + by_core[j % 2](i)) for j in range(n_hid) for i in range(n_ffn)
        ]
        return lax.ppermute(jnp.concatenate(values), ("hid", "ffn"), perm)

    def plus(left, right):
        return (left.astype(F32) + right.astype(F32)).astype(BF)

    first = jnp.where(c == 0, beside(f), around(f))
    second = jnp.where(c == 0, around(f), beside(f))
    across = n_ffn - 1 - beside(f)
    block = rows // n_ffn
    input_part = dot(deltas, weights, 1, 0).astype(BF)
    mixed_part = dot(hidden, down_eff, 1, 0).astype(BF).reshape(n_ffn, block, feats)
    got = swap([input_part, pick(mixed_part, first), pick(mixed_part, across)], (beside, around))
    input_sum = plus(input_part, got[:rows])
    own_sum = plus(pick(mixed_part, f), got[rows : rows + block])
    sent_sum = plus(pick(mixed_part, second), got[rows + block :])
    got = swap([input_sum, sent_sum], (around, beside))
    got, sums = lax.optimization_barrier((got, sums))
    tokens_grad = plus(input_sum, got[:rows])
    mixed = plus(own_sum, got[rows:])

    gate_grad = (sums[:own] * keep_gate.astype(F32)).astype(BF).T
    up_grad = (sums[own : 2 * own] * keep_up.astype(F32)).astype(BF).T
    down_grad = (sums[2 * own :] * keep_own_down.astype(F32)).astype(BF)
    return (mixed, tokens_grad, gate_grad, up_grad, down_grad)


def solution(mesh):
    in_specs = (
        P("tok", "hid"),
        P("hid", ("ffn", "tok")),
        P("hid", ("ffn", "tok")),
        P("ffn", "hid"),
        P(),
        P(),
        P(),
        P(("tok", "ffn"), "hid"),
    )
    out_specs = (
        P(("tok", "ffn"), "hid"),
        P("tok", "hid"),
        P("hid", ("ffn", "tok")),
        P("hid", ("ffn", "tok")),
        P(("ffn", "tok"), "hid"),
    )
    return jax.shard_map(body, mesh=mesh, in_specs=in_specs, out_specs=out_specs, check_vma=False)
```

```python
import jax
import jax.numpy as jnp
from jax import lax
from jax.experimental import pallas as pl
from jax.experimental.pallas import tpu as pltpu
from jax.sharding import PartitionSpec as P

BLOCK = 128
BF = jnp.bfloat16
F32 = jnp.float32


def dot(left, right, left_axis, right_axis):
    return lax.dot_general(
        left, right, (((left_axis,), (right_axis,)), ((), ())), preferred_element_type=F32
    )


def total(parts):
    return jnp.sum(parts.astype(F32), axis=0)


def pick(parts, index):
    return lax.dynamic_index_in_dim(parts, index, 0, keepdims=False)


def keep_rows(mask, row_first, row_blocks, col_first, col_blocks):
    part = lax.dynamic_slice(mask, (row_first, col_first), (row_blocks, col_blocks))
    return jnp.repeat(part.astype(BF), BLOCK, axis=1)


def activation_kernel(own, units, part_ref, out_ref):
    for k in range(units // own):
        at = 2 * own * k
        gate = total(part_ref[:, :, at : at + own])
        up = total(part_ref[:, :, at + own : at + 2 * own])
        hidden_grad = total(part_ref[:, :, 2 * units + own * k : 2 * units + own * (k + 1)])
        sigma = jax.nn.sigmoid(gate)
        out_ref[:, 2 * units + own * k : 2 * units + own * (k + 1)] = (gate * sigma * up).astype(BF)
        out_ref[:, at : at + own] = (
            hidden_grad * up * sigma * (1.0 + gate * (1.0 - sigma))
        ).astype(BF)
        out_ref[:, at + own : at + 2 * own] = (hidden_grad * gate * sigma).astype(BF)


def activation(own, units, parts):
    count = parts.shape[1]
    return pl.pallas_call(
        lambda *refs: activation_kernel(own, units, *refs),
        out_shape=jax.ShapeDtypeStruct((count, 3 * units), BF),
        in_specs=[pl.BlockSpec(memory_space=pltpu.VMEM)],
        out_specs=pl.BlockSpec(memory_space=pltpu.VMEM),
        compiler_params=pltpu.CompilerParams(vmem_limit_bytes=16 * 2**20),
        cost_estimate=pl.CostEstimate(
            flops=20 * count * units, bytes_accessed=30 * count * units, transcendentals=count * units
        ),
    )(parts)


def body(tokens, gate_weight, up_weight, down_weight, gate_mask, up_mask, down_mask, cotangent):
    n_tok, n_hid, n_ffn = (lax.axis_size(a) for a in ("tok", "hid", "ffn"))
    t, h, f = (lax.axis_index(a) for a in ("tok", "hid", "ffn"))
    rows, feats = tokens.shape
    units = down_weight.shape[0]
    own = units // n_tok
    feat_blocks, unit_blocks = feats // BLOCK, units // BLOCK
    n_line = n_hid // 2
    c = h % 2
    pairs = [[2 * i + j for j in range(2)] for i in range(n_line)]
    lines = [[2 * i + j for i in range(n_line)] for j in range(2)]

    def hop_hid(value, distance):
        return lax.ppermute(value, "hid", [(i, i ^ distance) for i in range(n_hid)])

    own_block = (f * units + t * own) // BLOCK
    keep_gate = keep_rows(gate_mask.T, own_block, 1, h * feat_blocks, feat_blocks)
    keep_up = keep_rows(up_mask.T, own_block, 1, h * feat_blocks, feat_blocks)
    keep_own_down = keep_rows(down_mask, own_block, 1, h * feat_blocks, feat_blocks)
    keep_down = keep_rows(down_mask, f * unit_blocks, unit_blocks, h * feat_blocks, feat_blocks)
    down_eff = (down_weight.reshape(unit_blocks, BLOCK, feats) * keep_down[:, None, :]).reshape(
        units, feats
    )

    spread = jnp.broadcast_to(
        jnp.concatenate([gate_weight.T, up_weight.T])[None], (n_tok, 2 * own, feats)
    )
    gathered = lax.all_to_all(spread, "tok", 0, 0)
    first_block = f * unit_blocks
    keep_both = jnp.stack(
        [
            keep_rows(mask.T, first_block, unit_blocks, h * feat_blocks, feat_blocks)
            for mask in (gate_mask, up_mask)
        ],
        axis=1,
    )
    keep_both = jnp.repeat(keep_both, n_tok // unit_blocks, axis=0)
    grad_rows = lax.all_gather(cotangent, "ffn", axis=0, tiled=True)

    def sum_cores(part):
        part = part.astype(BF).reshape(2, rows // 2, part.shape[1])
        half = pick(part, c).astype(F32) + hop_hid(pick(part, 1 - c), 1).astype(F32)
        return half.astype(BF).reshape(n_line, rows // n_hid, part.shape[2])

    grad_half = sum_cores(dot(grad_rows, down_eff, 1, 1))
    gathered, grad_half = lax.optimization_barrier((gathered, grad_half))
    weights = gathered.reshape(n_tok, 2, own, feats) * keep_both[:, :, None, :]
    weights = weights.reshape(2 * units, feats)
    both_half = sum_cores(dot(tokens, weights, 1, 1))
    def trade(value, by_core):
        return lax.ppermute(value, "hid", [(i, i ^ (2 * by_core[i % 2])) for i in range(n_hid)])

    z = h // 2
    halves = jnp.concatenate([both_half, grad_half], axis=2)
    near, far = z ^ jnp.where(c == 0, 2, 1), z ^ jnp.where(c == 0, 1, 2)
    got = trade(jnp.stack([pick(halves, near), pick(halves, z ^ 3)]), (2, 1))
    sent_sum = (pick(halves, far).astype(F32) + got[1].astype(F32)).astype(BF)
    parts = jnp.stack([pick(halves, z), got[0], trade(sent_sum, (1, 2))])
    acts = activation(own, units, parts)
    mine = lax.all_gather(acts, "hid", axis=0, tiled=True, axis_index_groups=lines)
    other = hop_hid(mine, 1)

    def in_order(first, last):
        halves = mine[:, first:last], other[:, first:last]
        return jnp.concatenate([jnp.where(c == k, *halves) for k in range(2)])

    deltas = in_order(0, 2 * units)
    hidden = in_order(2 * units, 3 * units)

    delta_term = dot(deltas, tokens, 0, 0).astype(BF).reshape(n_tok, 2 * own, feats)
    down_term = dot(hidden, grad_rows, 0, 0).astype(BF).reshape(n_tok, own, feats)
    terms = lax.all_to_all(jnp.concatenate([delta_term, down_term], axis=1), "tok", 0, 0)

    def gradient(kind, keep):
        own_terms = terms[:, kind * own : (kind + 1) * own]
        return (total(own_terms) * (1.0 / n_tok) * keep.astype(F32)).astype(BF)

    grads = [gradient(k, keep) for k, keep in enumerate((keep_gate, keep_up, keep_own_down))]

    def beside(i):
        return i ^ 1

    def around(i):
        return n_ffn - 1 - i

    def swap(values, by_core):
        perm = [
            (j * n_ffn + i, j * n_ffn + by_core[j % 2](i)) for j in range(n_hid) for i in range(n_ffn)
        ]
        return lax.ppermute(jnp.concatenate(values), ("hid", "ffn"), perm)

    def plus(left, right):
        return (left.astype(F32) + right.astype(F32)).astype(BF)

    first = jnp.where(c == 0, beside(f), around(f))
    second = jnp.where(c == 0, around(f), beside(f))
    across = n_ffn - 1 - beside(f)
    block = rows // n_ffn
    input_part = dot(deltas, weights, 1, 0).astype(BF)
    mixed_part = dot(hidden, down_eff, 1, 0).astype(BF).reshape(n_ffn, block, feats)
    got = swap([input_part, pick(mixed_part, first), pick(mixed_part, across)], (beside, around))
    input_sum = plus(input_part, got[:rows])
    own_sum = plus(pick(mixed_part, f), got[rows : rows + block])
    sent_sum = plus(pick(mixed_part, second), got[rows + block :])
    got = swap([input_sum, sent_sum], (around, beside))
    got, grads = lax.optimization_barrier((got, grads))
    tokens_grad = plus(input_sum, got[:rows])
    mixed = plus(own_sum, got[rows:])

    gate_grad, up_grad, down_grad = grads
    return (mixed, tokens_grad, gate_grad.T, up_grad.T, down_grad)


def solution(mesh):
    in_specs = (
        P("tok", "hid"),
        P("hid", ("ffn", "tok")),
        P("hid", ("ffn", "tok")),
        P("ffn", "hid"),
        P(),
        P(),
        P(),
        P(("tok", "ffn"), "hid"),
    )
    out_specs = (
        P(("tok", "ffn"), "hid"),
        P("tok", "hid"),
        P("hid", ("ffn", "tok")),
        P("hid", ("ffn", "tok")),
        P(("ffn", "tok"), "hid"),
    )
    return jax.shard_map(body, mesh=mesh, in_specs=in_specs, out_specs=out_specs, check_vma=False)
```
